32 devices in a mesh: dp: 8 (over y, x, core), mp: 4 (over z).
Axes of the slice: x: 2, y: 2, z: 4, core: 2. Of those that a mesh axis runs over, the one named last changes fastest.
Arguments:
- sample_grad: bfloat16 [1152, 8192], P('dp', 'mp'), may hold values from -3 to 3
- advantage: int32 [1152], P('dp'), may hold values from 1024 to 8191
- route_rows: int32 [8, 144], P('dp'), may hold values from 0 to 143, each once within a row
- route_count: int32 [8, 8], P('dp'), may hold values from 1 to 16, 80 in all within a row
- gate_pre: bfloat16 [1024, 16384], P('mp', 'dp'), may hold values from -5 to 5
- up_pre: bfloat16 [1024, 16384], P('mp', 'dp'), may hold values from -5 to 5
- down_weight: bfloat16 [16384, 8192], P('dp', 'mp'), may hold values from -0.046875 to 0.046875
Outputs:
- grad_down: float32 [16384, 8192], P('dp', 'mp')
- grad_gate: bfloat16 [1024, 16384], P('mp', 'dp')
- grad_up: bfloat16 [1024, 16384], P('mp', 'dp')
The draws below stay inside these ranges and needn't reach their ends.
Inputs may be any that keep to these rules, and one draw needn't show every extreme that they name: Each row of route_rows is a permutation of the sampler's 144 row numbers. `route_count`: each sampler sends every learner at least one row and 80 rows in all; in each sampler's row some learner receives exactly 16.
All inputs are finite; a program needn't handle non-finite values.
Results may differ from the reference program's by a relative error of at most 0.005.
Values may be sent and summed in bfloat16 or wider, within the bound.
A program may use at most 128 MiB of HBM per device.

```python
import math
import jax
import jax.numpy as jnp
import numpy as np
from jax import lax

D = 8192
FF = 16384
SLOTS = 128
S_DEV = 144
T_TOTAL = 1024
S_TOTAL = 1152
N_DP = 8


def with_ends(result, stream_key, least, high):
    spot = [jax.random.randint(jax.random.fold_in(stream_key, axis), (), 0, length) for axis, length in enumerate(result.shape)]
    widest = result.shape.index(max(result.shape))
    beside = spot[:widest] + [(spot[widest] + 1) % result.shape[widest]] + spot[widest + 1:]
    return result.at[tuple(spot)].set(least).at[tuple(beside)].set(high)


def block_levels(rng, extent, cuts, least, largest):
    def one(position, blocks):
        steps = jax.random.uniform(jax.random.fold_in(jax.random.fold_in(rng, 6), position), (blocks,), jnp.float32, least / len(cuts), largest / len(cuts))
        return jnp.repeat(jnp.exp(steps), extent[position] // blocks).reshape((-1,) + (1,) * (len(extent) - position - 1))

    gain = one(*cuts[0])
    for cut in cuts[1:]:
        gain = gain * one(*cut)
    return gain


def profile(amount, total, limit, skew):
    portions = [(1 << 20) // math.isqrt(standing ** skew) + 1 for standing in range(2, amount + 1)]
    surplus, given = total - limit - (amount - 1), [1] * (amount - 1)
    while surplus > 0:
        movable = [i for i in range(amount - 1) if given[i] < limit]
        pool, budget = sum([portions[i] for i in movable]), surplus
        for i in movable:
            addition = min(limit - given[i], max(1, budget * portions[i] // pool), surplus)
            given[i] = given[i] + addition
            surplus = surplus - addition
    return np.array([limit] + given)


def uneven(own_key, count, total, reach, lean):
    if count == 2:
        one = jax.random.randint(own_key, (), max(1, total - reach), min(reach, total - 1) + 1)
        return jnp.stack([one, total - one])
    sizes = jnp.asarray(profile(count, total, reach, lean), jnp.int32)
    couples = (count - 1) // 2
    donor, taker = sizes[1:1 + 2 * couples:2], sizes[2:2 + 2 * couples:2]
    slack = jnp.minimum(donor - 1, reach - taker)
    moved = jax.random.randint(jax.random.fold_in(own_key, 1), (couples,), 0, 1 << 20) % (slack + 1)
    sizes = sizes.at[1:1 + 2 * couples:2].set(donor - moved).at[2:2 + 2 * couples:2].set(taker + moved)
    return sizes[jax.random.permutation(jax.random.fold_in(own_key, 2), count)]


def gaussian(own_key, extent, deviation, reach, pieces=(), held_as=jnp.bfloat16):
    level = block_levels(own_key, extent, pieces, -0.22, 0.18) if pieces else 1.0
    drawn = jax.random.normal(own_key, extent, jnp.float32) * deviation * level
    return jnp.minimum(jnp.maximum(drawn, -reach), reach).astype(held_as)


def setup_inputs(seed: int = 0) -> dict:
    streams_of = jax.random.split(jax.random.key(seed), 8)
    return {
        "sample_grad": gaussian(streams_of[0], (S_TOTAL, D), 0.5, 3.0, ((0, 8), (1, 4))),
        "advantage": with_ends(jax.random.randint(streams_of[1], (S_TOTAL,), 1024, 8192), jax.random.fold_in(streams_of[1], 1), 1024, 8191).astype(jnp.int32),
        "route_rows": jax.vmap(lambda own: jax.random.permutation(own, S_DEV))(jax.random.split(streams_of[2], N_DP)).reshape((N_DP, S_DEV)).astype(jnp.int32),
        "route_count": jax.vmap(lambda own: uneven(own, N_DP, SLOTS * 5 // 8, SLOTS // N_DP, 2))(jax.random.split(streams_of[3], N_DP)).reshape((N_DP, N_DP)).astype(jnp.int32),
        "gate_pre": gaussian(streams_of[4], (T_TOTAL, FF), 1.0, 5.0, ((0, 4), (1, 8))),
        "up_pre": gaussian(streams_of[5], (T_TOTAL, FF), 1.0, 5.0, ((0, 4), (1, 8))),
        "down_weight": gaussian(streams_of[6], (FF, D), FF ** -0.5, 0.046875, ((0, 8), (1, 4))),
    }


def silu_parts(gate_in):
    sigmoid_val = jax.nn.sigmoid(gate_in)
    return gate_in * sigmoid_val, sigmoid_val * (1.0 + gate_in * (1.0 - sigmoid_val))


def reference(sample_grad, advantage, route_rows, route_count, gate_pre, up_pre, down_weight):
    weights = advantage.astype(jnp.float32) * (1.0 / 4096.0)
    scaled = (sample_grad.astype(jnp.float32) * weights[:, None]).astype(jnp.bfloat16)
    capacity = SLOTS // N_DP
    route_table = route_rows[:, :SLOTS].reshape(N_DP, N_DP, capacity)
    offsets = (jnp.arange(N_DP, dtype=jnp.int32) * S_DEV)[:, None, None]
    source_rows = jnp.transpose(route_table + offsets, (1, 0, 2)).reshape(-1).astype(jnp.int32)
    live_mask = jnp.arange(capacity, dtype=jnp.int32)[None, None, :] < route_count[:, :, None]
    live_mask = jnp.transpose(live_mask, (1, 0, 2)).reshape(-1)
    slot_rows = jnp.where(live_mask[:, None], scaled[source_rows], jnp.zeros((), jnp.bfloat16))
    gate_in = gate_pre.astype(jnp.float32)
    up_in = up_pre.astype(jnp.float32)
    activated, slopes = silu_parts(gate_in)
    hidden = (activated * up_in).astype(jnp.bfloat16)
    grad_down = lax.dot_general(hidden, slot_rows, (((0,), (0,)), ((), ())), preferred_element_type=jnp.float32)
    hidden_grad = lax.dot_general(slot_rows, down_weight, (((1,), (1,)), ((), ())), preferred_element_type=jnp.float32)
    grad_gate = (hidden_grad * up_in * slopes).astype(jnp.bfloat16)
    grad_up = (hidden_grad * activated).astype(jnp.bfloat16)
    return grad_down, grad_gate, grad_up
```

```python
import jax
import jax.numpy as jnp
from jax import lax
from jax.sharding import PartitionSpec as P

SLOTS = 128
LIVE = SLOTS * 5 // 8
SENT = LIVE + 16
SIXTEENTHS = (11, 12, 13, 16)


def dot(a, b, a_dim, b_dim):
    return lax.dot_general(a, b, (((a_dim,), (b_dim,)), ((), ())), preferred_element_type=jnp.float32)


def pick(mask, table):
    return dot(mask.astype(jnp.bfloat16), table, 1, 0).astype(jnp.bfloat16)


def iota(shape, axis):
    return lax.broadcasted_iota(jnp.int32, shape, axis)


def ends_of(counts):
    n = counts.shape[-1]
    return jnp.sum(jnp.where(iota((n, n), 0) <= iota((n, n), 1), counts[..., :, None], 0), axis=-2)


def shards(sample_grad, advantage, route_rows, route_count, gate_pre, up_pre, down_weight):
    learners, n = lax.axis_size("dp"), lax.axis_size("mp")
    me = lax.axis_index("mp")
    width = SLOTS // learners
    per = learners // n
    rows = gate_pre.shape[0]
    right = [(i, i + 1) for i in range(n - 1)]
    left = [(i + 1, i) for i in range(n - 1)]

    gate_in = gate_pre.astype(jnp.float32)
    up_in = up_pre.astype(jnp.float32)
    hidden = (gate_in * jax.nn.sigmoid(gate_in) * up_in).astype(jnp.bfloat16)

    weights = advantage.astype(jnp.float32) * (1.0 / 4096.0)
    scaled = (sample_grad.astype(jnp.float32) * weights[:, None]).astype(jnp.bfloat16)
    own_count = route_count[0]
    own_start = ends_of(own_count) - own_count
    spot = iota((learners, width), 1)
    place = jnp.where(spot < own_count[:, None], own_start[:, None] + spot, -1).reshape(-1)
    table = route_rows[0, :SLOTS]
    source = jnp.sum(jnp.where(iota((LIVE, SLOTS), 0) == place[None, :], table[None, :], 0), axis=1)
    packed = pick(source[:, None] == iota((LIVE, scaled.shape[0]), 1), scaled)
    tail = jnp.pad(own_count.astype(jnp.bfloat16)[None, :], ((0, SENT - LIVE - 1), (0, scaled.shape[1] - learners)))
    everything = lax.all_gather(jnp.concatenate([packed, tail]), "dp", axis=0, tiled=False)

    from_left = lax.ppermute(hidden, "mp", right)
    from_right = lax.ppermute(hidden, "mp", left)

    counts = everything[:, LIVE, :learners].astype(jnp.int32)
    everything = everything.reshape(learners * SENT, -1)
    ends = ends_of(counts)
    by_learner = counts.T.reshape(n, per * learners)
    rank_ends = ends_of(by_learner)
    totals = rank_ends[:, -1]
    rank_start = (rank_ends - by_learner).reshape(learners, learners)

    p = iota((learners, learners, SENT), 2)
    begin = (ends - counts).T[:, :, None]
    finish = ends.T[:, :, None]
    inside = (p >= begin) & (p < finish)
    to_block = jnp.sum(jnp.where(inside, iota(p.shape, 0) // per + 1, 0), axis=0).reshape(-1) - 1
    to_rank = jnp.sum(jnp.where(inside, rank_start[:, :, None] + p - begin, 0), axis=0).reshape(-1)

    c = iota((n, per * learners, width), 2)
    slot_rank = jnp.where(c < by_learner[:, :, None], rank_start.reshape(n, -1)[:, :, None] + c, -1).reshape(n, rows)

    order = [1, n - 1] + [t for t in range(2, n - 1)] + [0]
    first = 2

    def body(cap):
        def run(hidden, from_left, from_right, everything, to_block, to_rank, slot_rank, gate_pre, up_pre, down_weight):
            def mask_of(block):
                ranks = lax.dynamic_slice_in_dim(slot_rank, block, 1, 0)
                return iota((cap, rows), 0) == ranks

            own_mask = mask_of(me)
            kept = {0: pick(own_mask, hidden)}
            r_in = pick(mask_of((me - 1) % n), from_left)
            l_in = pick(mask_of((me + 1) % n), from_right)

            def slots_of(positions):
                held = [
                    (to_block == (me - t) % n)[None, :] & (iota((cap, to_rank.shape[0]), 0) == to_rank[None, :])
                    for t in positions
                ]
                return pick(jnp.concatenate(held), everything)

            slots_a = slots_of(order[:first])
            part_a = lax.optimization_barrier(dot(slots_a, down_weight, 1, 1))
            slots_b = slots_of(order[first:])
            part_b = lax.optimization_barrier(dot(slots_b, down_weight, 1, 1))
            partial = {}
            for i, t in enumerate(order):
                held = part_a if i < first else part_b
                at = (i if i < first else i - first) * cap
                partial[t] = held[at:at + cap]

            rights, lefts = {1: r_in}, {1: l_in}
            for step in range(2, n + 1):
                def load(came, position, adds):
                    own = jnp.where(adds, partial[position], 0.0)
                    return (came.astype(jnp.float32) + own).astype(jnp.bfloat16)

                r_out = load(jnp.where(me > 0, rights[step - 1], 0), step - 1, step >= me + 2)
                l_out = load(jnp.where(me < n - 1, lefts[step - 1], 0), n + 1 - step, step >= n - me + 1)
                rights[step] = lax.ppermute(r_out, "mp", right)
                lefts[step] = lax.ppermute(l_out, "mp", left)
            for t in range(1, n):
                kept[t] = jnp.where(me >= t, rights[t], lefts[n - t])
            hidden_all = jnp.concatenate([kept[t] for t in order])
            grad_down = dot(hidden_all, jnp.concatenate([slots_a, slots_b]), 0, 0)

            hidden_grad = partial[0] + rights[n].astype(jnp.float32) + lefts[n].astype(jnp.float32)
            gate_in = pick(own_mask, gate_pre).astype(jnp.float32)
            up_in = pick(own_mask, up_pre).astype(jnp.float32)
            s = jax.nn.sigmoid(gate_in)
            grad_gate = (hidden_grad * up_in * (s * (1.0 + gate_in * (1.0 - s)))).astype(jnp.bfloat16)
            grad_up = (hidden_grad * (gate_in * s)).astype(jnp.bfloat16)
            spread = own_mask.astype(jnp.bfloat16)
            grad_gate = dot(spread, grad_gate, 0, 0).astype(jnp.bfloat16)
            grad_up = dot(spread, grad_up, 0, 0).astype(jnp.bfloat16)
            return grad_down, grad_gate, grad_up

        return run

    caps = [rows * sixteenths // 16 for sixteenths in SIXTEENTHS]
    most = jnp.max(totals)
    choice = sum((most > cap).astype(jnp.int32) for cap in caps[:-1])
    return lax.switch(
        choice, [body(cap) for cap in caps],
        hidden, from_left, from_right, everything, to_block, to_rank, slot_rank, gate_pre, up_pre, down_weight,
    )


def solution(mesh):
    placed = (
        P("dp", "mp"),
        P("dp"),
        P("dp", None),
        P("dp", None),
        P("mp", "dp"),
        P("mp", "dp"),
        P("dp", "mp"),
    )
    return jax.shard_map(
        shards,
        mesh=mesh,
        in_specs=placed,
        out_specs=(P("dp", "mp"), P("mp", "dp"), P("mp", "dp")),
        check_vma=False,
    )
```

```python
import functools

import jax
import jax.numpy as jnp
from jax import lax
from jax.experimental import pallas as pl
from jax.experimental.pallas import tpu as pltpu
from jax.sharding import PartitionSpec as P

SLOTS = 128
LIVE = SLOTS * 5 // 8
SENT = LIVE + 16
SIXTEENTHS = (11, 12, 13, 16)
LINE = True


def dot(a, b, a_dim, b_dim):
    return lax.dot_general(a, b, (((a_dim,), (b_dim,)), ((), ())), preferred_element_type=jnp.float32)


def pick(mask, table):
    return dot(mask.astype(jnp.bfloat16), table, 1, 0).astype(jnp.bfloat16)


def iota(shape, axis):
    return lax.broadcasted_iota(jnp.int32, shape, axis)


def ends_of(counts):
    n = counts.shape[-1]
    return jnp.sum(jnp.where(iota((n, n), 0) <= iota((n, n), 1), counts[..., :, None], 0), axis=-2)


MESH = pl.DeviceIdType.MESH


def remote(src, dst, sends, recvs, at, axis, target):
    return pltpu.make_async_remote_copy(
        src_ref=src, dst_ref=dst, send_sem=sends.at[at], recv_sem=recvs.at[at],
        device_id={axis: target}, device_id_type=MESH,
    )


def spread_kernel(peers, n, x_ref, h_ref, all_ref, fl_ref, fr_ref, sends, recvs, z_sends, z_recvs, own_sem):
    k, me = lax.axis_index("dp"), lax.axis_index("mp")
    bits = peers.bit_length() - 1
    barrier = pltpu.get_barrier_semaphore()

    def flip(i, b):
        return i + (1 << b) * (1 - 2 * ((i // (1 << b)) % 2))

    for b in range(bits):
        pl.semaphore_signal(barrier, inc=1, device_id={"dp": flip(k, b)}, device_id_type=MESH)
    for t in (1, n - 1):
        pl.semaphore_signal(barrier, inc=1, device_id={"mp": lax.rem(me + t, n)}, device_id_type=MESH)
    pl.semaphore_wait(barrier, bits + 2)

    to_right = remote(h_ref, fl_ref, z_sends, z_recvs, 0, "mp", lax.rem(me + 1, n))
    to_left = remote(h_ref, fr_ref, z_sends, z_recvs, 1, "mp", lax.rem(me + n - 1, n))

    @pl.when(me < n - 1)
    def _():
        to_right.start()

    @pl.when(me > 0)
    def _():
        to_left.start()

    own = pltpu.make_async_copy(x_ref, all_ref.at[k], own_sem)
    own.start()
    half = x_ref.shape[0] // 2
    orders = [list(range(bits - 1, -1, -1)), list(range(bits - 2, 0, -1)) + [bits - 1, 0]]
    plans = []
    for h, order in enumerate(orders):
        at, seen, stages = h * (peers - 1), [()], []
        for b in order:
            stage = []
            for flips in seen:
                stage.append((at, flips, b))
                at += 1
            stages.append(stage)
            seen = seen + [flips + (b,) for flips in seen]
        plans.append(stages)

    def copy(h, at, flips, b):
        rows = pl.ds(h * half, half)
        source = k
        for f in flips:
            source = flip(source, f)
        src = x_ref.at[rows] if not flips else all_ref.at[source, rows]
        return remote(src, all_ref.at[source, rows], sends, recvs, at, "dp", flip(k, b))

    def arrival(h, at, flips, b):
        rows = pl.ds(h * half, half)
        source = flip(k, b)
        for f in flips:
            source = flip(source, f)
        here = all_ref.at[source, rows]
        return remote(here, here, sends, recvs, at, "dp", flip(k, b))

    for i in range(bits):
        for h in range(2):
            for piece in plans[h][i]:
                copy(h, *piece).start()
        for h in range(2):
            for piece in plans[h][i]:
                arrival(h, *piece).wait_recv()
    for i in range(bits):
        for h in range(2):
            for piece in plans[h][i]:
                copy(h, *piece).wait_send()
    own.wait()

    @pl.when(me < n - 1)
    def _():
        to_right.wait_send()
        to_left.wait_recv()

    @pl.when(me > 0)
    def _():
        to_left.wait_send()
        to_right.wait_recv()


def spread(packed, hidden, peers, n):
    hbm = pl.BlockSpec(memory_space=pl.ANY)
    count = 2 * (peers - 1)
    dma = pltpu.SemaphoreType.DMA
    return pl.pallas_call(
        functools.partial(spread_kernel, peers, n),
        out_shape=(
            jax.ShapeDtypeStruct((peers,) + packed.shape, packed.dtype),
            jax.ShapeDtypeStruct(hidden.shape, hidden.dtype),
            jax.ShapeDtypeStruct(hidden.shape, hidden.dtype),
        ),
        in_specs=[hbm] * 2,
        out_specs=(hbm,) * 3,
        scratch_shapes=[dma((count,)), dma((count,)), dma((2,)), dma((2,)), dma(())],
        compiler_params=pltpu.CompilerParams(collective_id=0, has_side_effects=True),
    )(packed, hidden)


def line_kernel(n, pieces, r_in, l_in, r_parts, l_parts, rights, lefts, r_out, l_out, sends, recvs):
    me = lax.axis_index("mp")
    barrier = pltpu.get_barrier_semaphore()
    for t in (1, n - 1):
        pl.semaphore_signal(barrier, inc=1, device_id={"mp": lax.rem(me + t, n)}, device_id_type=MESH)
    pl.semaphore_wait(barrier, 2)

    @pl.when(me == 0)
    def _():
        rights[...] = jnp.zeros_like(rights)

    @pl.when(me == n - 1)
    def _():
        lefts[...] = jnp.zeros_like(lefts)

    sides = (
        (r_in, r_parts, rights, r_out, me, me + 1),
        (l_in, l_parts, lefts, l_out, n - 1 - me, me + n - 1),
    )

    def piece(d, s, q):
        _, _, landing, held, _, to = sides[d]
        low, size = pieces[q]
        rows = pl.ds(low, size)
        at = (d * (n - 2) + s) * len(pieces) + q
        return remote(held.at[s, rows], landing.at[s, rows], sends, recvs, at, "mp", lax.rem(to, n))

    for s in range(n - 2):
        for q, (low, size) in enumerate(pieces):
            rows = pl.ds(low, size)
            for d, (came, parts, landing, held, seat, _) in enumerate(sides):
                if s:
                    @pl.when(seat > 0)
                    def _():
                        piece(d, s - 1, q).wait_recv()

                @pl.when(seat < n - 1)
                def _():
                    adds = (s >= seat).astype(jnp.float32) if s else (seat == 0).astype(jnp.float32)
                    before = landing[s - 1, rows] if s else came[rows]
                    total = before.astype(jnp.float32) + parts[s, rows] * adds
                    held[s, rows] = total.astype(held.dtype)
                    piece(d, s, q).start()
    for s in range(n - 2):
        for q in range(len(pieces)):
            for d in range(2):
                seat = sides[d][4]
                if s == n - 3:
                    @pl.when(seat > 0)
                    def _():
                        piece(d, s, q).wait_recv()

                @pl.when(seat < n - 1)
                def _():
                    piece(d, s, q).wait_send()


def line(number, n, r_in, l_in, r_parts, l_parts):
    cap, cols = r_in.shape
    units, many = cap // 16, 3
    cuts = [16 * (units * q // many) for q in range(many + 1)]
    pieces = [(a, b - a) for a, b in zip(cuts[:-1], cuts[1:])]
    vmem = pl.BlockSpec(memory_space=pltpu.VMEM)
    count = 2 * (n - 2) * many
    blocks = (n - 2, cap, cols)
    shape = jax.ShapeDtypeStruct(blocks, r_in.dtype)
    return pl.pallas_call(
        functools.partial(line_kernel, n, pieces),
        out_shape=(shape, shape),
        in_specs=[vmem] * 4,
        out_specs=(vmem, vmem),
        scratch_shapes=[
            pltpu.VMEM(blocks, r_in.dtype), pltpu.VMEM(blocks, r_in.dtype),
            pltpu.SemaphoreType.DMA((count,)), pltpu.SemaphoreType.DMA((count,)),
        ],
        compiler_params=pltpu.CompilerParams(
            collective_id=number, has_side_effects=True, vmem_limit_bytes=44 << 20
        ),
    )(r_in, l_in, r_parts, l_parts)


def shards(sample_grad, advantage, route_rows, route_count, gate_pre, up_pre, down_weight):
    learners, n = lax.axis_size("dp"), lax.axis_size("mp")
    me = lax.axis_index("mp")
    width = SLOTS // learners
    per = learners // n
    rows = gate_pre.shape[0]
    right = [(i, i + 1) for i in range(n - 1)]
    left = [(i + 1, i) for i in range(n - 1)]

    gate_in = gate_pre.astype(jnp.float32)
    up_in = up_pre.astype(jnp.float32)
    hidden = (gate_in * jax.nn.sigmoid(gate_in) * up_in).astype(jnp.bfloat16)

    weights = advantage.astype(jnp.float32) * (1.0 / 4096.0)
    scaled = (sample_grad.astype(jnp.float32) * weights[:, None]).astype(jnp.bfloat16)
    own_count = route_count[0]
    own_start = ends_of(own_count) - own_count
    spot = iota((learners, width), 1)
    place = jnp.where(spot < own_count[:, None], own_start[:, None] + spot, -1).reshape(-1)
    table = route_rows[0, :SLOTS]
    source = jnp.sum(jnp.where(iota((LIVE, SLOTS), 0) == place[None, :], table[None, :], 0), axis=1)
    packed = pick(source[:, None] == iota((LIVE, scaled.shape[0]), 1), scaled)
    tail = jnp.pad(own_count.astype(jnp.bfloat16)[None, :], ((0, SENT - LIVE - 1), (0, scaled.shape[1] - learners)))
    everything, from_left, from_right = spread(jnp.concatenate([packed, tail]), hidden, learners, n)

    counts = everything[:, LIVE, :learners].astype(jnp.int32)
    everything = everything.reshape(learners * SENT, -1)
    ends = ends_of(counts)
    by_learner = counts.T.reshape(n, per * learners)
    rank_ends = ends_of(by_learner)
    totals = rank_ends[:, -1]
    rank_start = (rank_ends - by_learner).reshape(learners, learners)

    p = iota((learners, learners, SENT), 2)
    begin = (ends - counts).T[:, :, None]
    finish = ends.T[:, :, None]
    inside = (p >= begin) & (p < finish)
    to_block = jnp.sum(jnp.where(inside, iota(p.shape, 0) // per + 1, 0), axis=0).reshape(-1) - 1
    to_rank = jnp.sum(jnp.where(inside, rank_start[:, :, None] + p - begin, 0), axis=0).reshape(-1)

    c = iota((n, per * learners, width), 2)
    slot_rank = jnp.where(c < by_learner[:, :, None], rank_start.reshape(n, -1)[:, :, None] + c, -1).reshape(n, rows)

    order = [1, n - 1] + [t for t in range(2, n - 1)] + [0]
    first = 2

    def body(number, cap):
        def run(hidden, from_left, from_right, everything, to_block, to_rank, slot_rank, gate_pre, up_pre, down_weight):
            def mask_of(block):
                ranks = lax.dynamic_slice_in_dim(slot_rank, block, 1, 0)
                return iota((cap, rows), 0) == ranks

            own_mask = mask_of(me)
            kept = {0: pick(own_mask, hidden)}
            r_in = pick(mask_of((me - 1) % n), from_left)
            l_in = pick(mask_of((me + 1) % n), from_right)

            def slots_of(positions):
                held = [
                    (to_block == (me - t) % n)[None, :] & (iota((cap, to_rank.shape[0]), 0) == to_rank[None, :])
                    for t in positions
                ]
                return pick(jnp.concatenate(held), everything)

            slots_a = slots_of(order[:first])
            part_a = lax.optimization_barrier(dot(slots_a, down_weight, 1, 1))
            slots_b = slots_of(order[first:])
            part_b = lax.optimization_barrier(dot(slots_b, down_weight, 1, 1))
            partial = {}
            for i, t in enumerate(order):
                held = part_a if i < first else part_b
                at = (i if i < first else i - first) * cap
                partial[t] = held[at:at + cap]

            def load(came, position, adds):
                own = jnp.where(adds, partial[position], 0.0)
                return (came.astype(jnp.float32) + own).astype(jnp.bfloat16)

            rights, lefts = {1: r_in}, {1: l_in}
            if LINE:
                r_parts = jnp.stack([partial[t] for t in range(1, n - 1)])
                l_parts = jnp.stack([partial[n - t] for t in range(1, n - 1)])
                r_all, l_all = line(number + 1, n, jnp.where(me > 0, r_in, 0), jnp.where(me < n - 1, l_in, 0), r_parts, l_parts)
                for step in range(2, n):
                    rights[step], lefts[step] = r_all[step - 2], l_all[step - 2]
            for step in range(n if LINE else 2, n + 1):
                r_out = load(jnp.where(me > 0, rights[step - 1], 0), step - 1, step >= me + 2)
                l_out = load(jnp.where(me < n - 1, lefts[step - 1], 0), n + 1 - step, step >= n - me + 1)
                rights[step] = lax.ppermute(r_out, "mp", right)
                lefts[step] = lax.ppermute(l_out, "mp", left)
            for t in range(1, n):
                kept[t] = jnp.where(me >= t, rights[t], lefts[n - t])
            hidden_all = jnp.concatenate([kept[t] for t in order])
            grad_down = dot(hidden_all, jnp.concatenate([slots_a, slots_b]), 0, 0)

            hidden_grad = partial[0] + rights[n].astype(jnp.float32) + lefts[n].astype(jnp.float32)
            gate_in = pick(own_mask, gate_pre).astype(jnp.float32)
            up_in = pick(own_mask, up_pre).astype(jnp.float32)
            s = jax.nn.sigmoid(gate_in)
            grad_gate = (hidden_grad * up_in * (s * (1.0 + gate_in * (1.0 - s)))).astype(jnp.bfloat16)
            grad_up = (hidden_grad * (gate_in * s)).astype(jnp.bfloat16)
            spread = own_mask.astype(jnp.bfloat16)
            grad_gate = dot(spread, grad_gate, 0, 0).astype(jnp.bfloat16)
            grad_up = dot(spread, grad_up, 0, 0).astype(jnp.bfloat16)
            return grad_down, grad_gate, grad_up

        return run

    caps = [rows * sixteenths // 16 for sixteenths in SIXTEENTHS]
    most = jnp.max(totals)
    choice = sum((most > cap).astype(jnp.int32) for cap in caps[:-1])
    return lax.switch(
        choice, [body(number, cap) for number, cap in enumerate(caps)],
        hidden, from_left, from_right, everything, to_block, to_rank, slot_rank, gate_pre, up_pre, down_weight,
    )


def solution(mesh):
    placed = (
        P("dp", "mp"),
        P("dp"),
        P("dp", None),
        P("dp", None),
        P("mp", "dp"),
        P("mp", "dp"),
        P("dp", "mp"),
    )
    return jax.shard_map(
        shards,
        mesh=mesh,
        in_specs=placed,
        out_specs=(P("dp", "mp"), P("mp", "dp"), P("mp", "dp")),
        check_vma=False,
    )
```

```python
import functools

import jax
import jax.numpy as jnp
from jax import lax
from jax.experimental import pallas as pl
from jax.experimental.pallas import tpu as pltpu
from jax.sharding import PartitionSpec as P

SLOTS = 128
LIVE = SLOTS * 5 // 8
SENT = LIVE + 16
SIXTEENTHS = (16,)
LINE = True


def dot(a, b, a_dim, b_dim):
    return lax.dot_general(a, b, (((a_dim,), (b_dim,)), ((), ())), preferred_element_type=jnp.float32)


def pick(mask, table):
    return dot(mask.astype(jnp.bfloat16), table, 1, 0).astype(jnp.bfloat16)


def iota(shape, axis):
    return lax.broadcasted_iota(jnp.int32, shape, axis)


def ends_of(counts):
    n = counts.shape[-1]
    return jnp.sum(jnp.where(iota((n, n), 0) <= iota((n, n), 1), counts[..., :, None], 0), axis=-2)


MESH = pl.DeviceIdType.MESH


def remote(src, dst, sends, recvs, at, axis, target):
    return pltpu.make_async_remote_copy(
        src_ref=src, dst_ref=dst, send_sem=sends.at[at], recv_sem=recvs.at[at],
        device_id={axis: target}, device_id_type=MESH,
    )


def spread_kernel(peers, n, x_ref, h_ref, all_ref, fl_ref, fr_ref, sends, recvs, z_sends, z_recvs, own_sem):
    k, me = lax.axis_index("dp"), lax.axis_index("mp")
    bits = peers.bit_length() - 1
    barrier = pltpu.get_barrier_semaphore()

    def flip(i, b):
        return i + (1 << b) * (1 - 2 * ((i // (1 << b)) % 2))

    for b in range(bits):
        pl.semaphore_signal(barrier, inc=1, device_id={"dp": flip(k, b)}, device_id_type=MESH)
    for t in (1, n - 1):
        pl.semaphore_signal(barrier, inc=1, device_id={"mp": lax.rem(me + t, n)}, device_id_type=MESH)
    pl.semaphore_wait(barrier, bits + 2)

    to_right = remote(h_ref, fl_ref, z_sends, z_recvs, 0, "mp", lax.rem(me + 1, n))
    to_left = remote(h_ref, fr_ref, z_sends, z_recvs, 1, "mp", lax.rem(me + n - 1, n))

    @pl.when(me < n - 1)
    def _():
        to_right.start()

    @pl.when(me > 0)
    def _():
        to_left.start()

    own = pltpu.make_async_copy(x_ref, all_ref.at[k], own_sem)
    own.start()
    half = x_ref.shape[0] // 2
    orders = [list(range(bits - 1, -1, -1)), list(range(bits - 2, 0, -1)) + [bits - 1, 0]]
    plans = []
    for h, order in enumerate(orders):
        at, seen, stages = h * (peers - 1), [()], []
        for b in order:
            stage = []
            for flips in seen:
                stage.append((at, flips, b))
                at += 1
            stages.append(stage)
            seen = seen + [flips + (b,) for flips in seen]
        plans.append(stages)

    def copy(h, at, flips, b):
        rows = pl.ds(h * half, half)
        source = k
        for f in flips:
            source = flip(source, f)
        src = x_ref.at[rows] if not flips else all_ref.at[source, rows]
        return remote(src, all_ref.at[source, rows], sends, recvs, at, "dp", flip(k, b))

    def arrival(h, at, flips, b):
        rows = pl.ds(h * half, half)
        source = flip(k, b)
        for f in flips:
            source = flip(source, f)
        here = all_ref.at[source, rows]
        return remote(here, here, sends, recvs, at, "dp", flip(k, b))

    for i in range(bits):
        for h in range(2):
            for piece in plans[h][i]:
                copy(h, *piece).start()
        for h in range(2):
            for piece in plans[h][i]:
                arrival(h, *piece).wait_recv()
    for i in range(bits):
        for h in range(2):
            for piece in plans[h][i]:
                copy(h, *piece).wait_send()
    own.wait()

    @pl.when(me < n - 1)
    def _():
        to_right.wait_send()
        to_left.wait_recv()

    @pl.when(me > 0)
    def _():
        to_left.wait_send()
        to_right.wait_recv()


def spread(packed, hidden, peers, n):
    hbm = pl.BlockSpec(memory_space=pl.ANY)
    count = 2 * (peers - 1)
    dma = pltpu.SemaphoreType.DMA
    return pl.pallas_call(
        functools.partial(spread_kernel, peers, n),
        out_shape=(
            jax.ShapeDtypeStruct((peers,) + packed.shape, packed.dtype),
            jax.ShapeDtypeStruct(hidden.shape, hidden.dtype),
            jax.ShapeDtypeStruct(hidden.shape, hidden.dtype),
        ),
        in_specs=[hbm] * 2,
        out_specs=(hbm,) * 3,
        scratch_shapes=[dma((count,)), dma((count,)), dma((2,)), dma((2,)), dma(())],
        compiler_params=pltpu.CompilerParams(collective_id=0, has_side_effects=True),
    )(packed, hidden)


def line_kernel(n, pieces, r_in, l_in, r_parts, l_parts, rights, lefts, r_out, l_out, sends, recvs):
    me = lax.axis_index("mp")
    barrier = pltpu.get_barrier_semaphore()
    for t in (1, n - 1):
        pl.semaphore_signal(barrier, inc=1, device_id={"mp": lax.rem(me + t, n)}, device_id_type=MESH)
    pl.semaphore_wait(barrier, 2)

    @pl.when(me == 0)
    def _():
        rights[...] = jnp.zeros_like(rights)

    @pl.when(me == n - 1)
    def _():
        lefts[...] = jnp.zeros_like(lefts)

    sides = (
        (r_in, r_parts, rights, r_out, me, me + 1),
        (l_in, l_parts, lefts, l_out, n - 1 - me, me + n - 1),
    )

    def piece(d, s, q):
        _, _, landing, held, _, to = sides[d]
        low, size = pieces[q]
        rows = pl.ds(low, size)
        at = (d * (n - 2) + s) * len(pieces) + q
        return remote(held.at[s, rows], landing.at[s, rows], sends, recvs, at, "mp", lax.rem(to, n))

    for s in range(n - 2):
        for q, (low, size) in enumerate(pieces):
            rows = pl.ds(low, size)
            for d, (came, parts, landing, held, seat, _) in enumerate(sides):
                if s:
                    @pl.when(seat > 0)
                    def _():
                        piece(d, s - 1, q).wait_recv()

                @pl.when(seat < n - 1)
                def _():
                    adds = (s >= seat).astype(jnp.float32) if s else (seat == 0).astype(jnp.float32)
                    before = landing[s - 1, rows] if s else came[rows]
                    total = before.astype(jnp.float32) + parts[s, rows] * adds
                    held[s, rows] = total.astype(held.dtype)
                    piece(d, s, q).start()
    for s in range(n - 2):
        for q in range(len(pieces)):
            for d in range(2):
                seat = sides[d][4]
                if s == n - 3:
                    @pl.when(seat > 0)
                    def _():
                        piece(d, s, q).wait_recv()

                @pl.when(seat < n - 1)
                def _():
                    piece(d, s, q).wait_send()


def line(number, n, r_in, l_in, r_parts, l_parts):
    cap, cols = r_in.shape
    units, many = cap // 16, 3
    cuts = [16 * (units * q // many) for q in range(many + 1)]
    pieces = [(a, b - a) for a, b in zip(cuts[:-1], cuts[1:])]
    vmem = pl.BlockSpec(memory_space=pltpu.VMEM)
    count = 2 * (n - 2) * many
    blocks = (n - 2, cap, cols)
    shape = jax.ShapeDtypeStruct(blocks, r_in.dtype)
    return pl.pallas_call(
        functools.partial(line_kernel, n, pieces),
        out_shape=(shape, shape),
        in_specs=[vmem] * 4,
        out_specs=(vmem, vmem),
        scratch_shapes=[
            pltpu.VMEM(blocks, r_in.dtype), pltpu.VMEM(blocks, r_in.dtype),
            pltpu.SemaphoreType.DMA((count,)), pltpu.SemaphoreType.DMA((count,)),
        ],
        compiler_params=pltpu.CompilerParams(
            collective_id=number, has_side_effects=True, vmem_limit_bytes=44 << 20
        ),
    )(r_in, l_in, r_parts, l_parts)


def shards(sample_grad, advantage, route_rows, route_count, gate_pre, up_pre, down_weight):
    learners, n = lax.axis_size("dp"), lax.axis_size("mp")
    me = lax.axis_index("mp")
    width = SLOTS // learners
    per = learners // n
    rows = gate_pre.shape[0]
    right = [(i, i + 1) for i in range(n - 1)]
    left = [(i + 1, i) for i in range(n - 1)]

    gate_in = gate_pre.astype(jnp.float32)
    up_in = up_pre.astype(jnp.float32)
    hidden = (gate_in * jax.nn.sigmoid(gate_in) * up_in).astype(jnp.bfloat16)

    weights = advantage.astype(jnp.float32) * (1.0 / 4096.0)
    scaled = (sample_grad.astype(jnp.float32) * weights[:, None]).astype(jnp.bfloat16)
    own_count = route_count[0]
    own_start = ends_of(own_count) - own_count
    spot = iota((learners, width), 1)
    place = jnp.where(spot < own_count[:, None], own_start[:, None] + spot, -1).reshape(-1)
    table = route_rows[0, :SLOTS]
    source = jnp.sum(jnp.where(iota((LIVE, SLOTS), 0) == place[None, :], table[None, :], 0), axis=1)
    packed = pick(source[:, None] == iota((LIVE, scaled.shape[0]), 1), scaled)
    tail = jnp.pad(own_count.astype(jnp.bfloat16)[None, :], ((0, SENT - LIVE - 1), (0, scaled.shape[1] - learners)))
    everything, from_left, from_right = spread(jnp.concatenate([packed, tail]), hidden, learners, n)

    counts = everything[:, LIVE, :learners].astype(jnp.int32)
    everything = everything.reshape(learners * SENT, -1)
    ends = ends_of(counts)
    by_learner = counts.T.reshape(n, per * learners)
    rank_ends = ends_of(by_learner)
    totals = rank_ends[:, -1]
    rank_start = (rank_ends - by_learner).reshape(learners, learners)

    p = iota((learners, learners, SENT), 2)
    begin = (ends - counts).T[:, :, None]
    finish = ends.T[:, :, None]
    inside = (p >= begin) & (p < finish)
    to_block = jnp.sum(jnp.where(inside, iota(p.shape, 0) // per + 1, 0), axis=0).reshape(-1) - 1
    to_rank = jnp.sum(jnp.where(inside, rank_start[:, :, None] + p - begin, 0), axis=0).reshape(-1)

    c = iota((n, per * learners, width), 2)
    slot_rank = jnp.where(c < by_learner[:, :, None], rank_start.reshape(n, -1)[:, :, None] + c, -1).reshape(n, rows)

    order = [1, n - 1] + [t for t in range(2, n - 1)] + [0]
    first = 2

    def body(number, cap):
        def run(hidden, from_left, from_right, everything, to_block, to_rank, slot_rank, gate_pre, up_pre, down_weight):
            def mask_of(block):
                ranks = lax.dynamic_slice_in_dim(slot_rank, block, 1, 0)
                return iota((cap, rows), 0) == ranks

            own_mask = mask_of(me)
            kept = {0: pick(own_mask, hidden)}
            r_in = pick(mask_of((me - 1) % n), from_left)
            l_in = pick(mask_of((me + 1) % n), from_right)

            def slots_of(positions):
                held = [
                    (to_block == (me - t) % n)[None, :] & (iota((cap, to_rank.shape[0]), 0) == to_rank[None, :])
                    for t in positions
                ]
                return pick(jnp.concatenate(held), everything)

            slots_a = slots_of(order[:first])
            part_a = lax.optimization_barrier(dot(slots_a, down_weight, 1, 1))
            slots_b = slots_of(order[first:])
            part_b = lax.optimization_barrier(dot(slots_b, down_weight, 1, 1))
            partial = {}
            for i, t in enumerate(order):
                held = part_a if i < first else part_b
                at = (i if i < first else i - first) * cap
                partial[t] = held[at:at + cap]

            def load(came, position, adds):
                own = jnp.where(adds, partial[position], 0.0)
                return (came.astype(jnp.float32) + own).astype(jnp.bfloat16)

            rights, lefts = {1: r_in}, {1: l_in}
            if LINE:
                r_parts = jnp.stack([partial[t] for t in range(1, n - 1)])
                l_parts = jnp.stack([partial[n - t] for t in range(1, n - 1)])
                r_all, l_all = line(number + 1, n, jnp.where(me > 0, r_in, 0), jnp.where(me < n - 1, l_in, 0), r_parts, l_parts)
                for step in range(2, n):
                    rights[step], lefts[step] = r_all[step - 2], l_all[step - 2]
            for step in range(n if LINE else 2, n + 1):
                r_out = load(jnp.where(me > 0, rights[step - 1], 0), step - 1, step >= me + 2)
                l_out = load(jnp.where(me < n - 1, lefts[step - 1], 0), n + 1 - step, step >= n - me + 1)
                rights[step] = lax.ppermute(r_out, "mp", right)
                lefts[step] = lax.ppermute(l_out, "mp", left)
            for t in range(1, n):
                kept[t] = jnp.where(me >= t, rights[t], lefts[n - t])
            hidden_all = jnp.concatenate([kept[t] for t in order])
            grad_down = dot(hidden_all, jnp.concatenate([slots_a, slots_b]), 0, 0)

            hidden_grad = partial[0] + rights[n].astype(jnp.float32) + lefts[n].astype(jnp.float32)
            gate_in = pick(own_mask, gate_pre).astype(jnp.float32)
            up_in = pick(own_mask, up_pre).astype(jnp.float32)
            s = jax.nn.sigmoid(gate_in)
            grad_gate = (hidden_grad * up_in * (s * (1.0 + gate_in * (1.0 - s)))).astype(jnp.bfloat16)
            grad_up = (hidden_grad * (gate_in * s)).astype(jnp.bfloat16)
            spread = own_mask.astype(jnp.bfloat16)
            grad_gate = dot(spread, grad_gate, 0, 0).astype(jnp.bfloat16)
            grad_up = dot(spread, grad_up, 0, 0).astype(jnp.bfloat16)
            return grad_down, grad_gate, grad_up

        return run

    caps = [rows * sixteenths // 16 for sixteenths in SIXTEENTHS]
    most = jnp.max(totals)
    choice = sum((most > cap).astype(jnp.int32) for cap in caps[:-1])
    return lax.switch(
        choice, [body(number, cap) for number, cap in enumerate(caps)],
        hidden, from_left, from_right, everything, to_block, to_rank, slot_rank, gate_pre, up_pre, down_weight,
    )


def solution(mesh):
    placed = (
        P("dp", "mp"),
        P("dp"),
        P("dp", None),
        P("dp", None),
        P("mp", "dp"),
        P("mp", "dp"),
        P("dp", "mp"),
    )
    return jax.shard_map(
        shards,
        mesh=mesh,
        in_specs=placed,
        out_specs=(P("dp", "mp"), P("mp", "dp"), P("mp", "dp")),
        check_vma=False,
    )
```

```python
import functools

import jax
import jax.numpy as jnp
from jax import lax
from jax.experimental import pallas as pl
from jax.experimental.pallas import tpu as pltpu
from jax.sharding import PartitionSpec as P

SLOTS = 128
LIVE = SLOTS * 5 // 8
SENT = LIVE + 16
LINE = True


def dot(a, b, a_dim, b_dim):
    return lax.dot_general(a, b, (((a_dim,), (b_dim,)), ((), ())), preferred_element_type=jnp.float32)


def pick(mask, table):
    return dot(mask.astype(jnp.bfloat16), table, 1, 0).astype(jnp.bfloat16)


def iota(shape, axis):
    return lax.broadcasted_iota(jnp.int32, shape, axis)


def ends_of(counts):
    n = counts.shape[-1]
    return jnp.sum(jnp.where(iota((n, n), 0) <= iota((n, n), 1), counts[..., :, None], 0), axis=-2)


MESH = pl.DeviceIdType.MESH


def remote(src, dst, sends, recvs, at, axis, target):
    return pltpu.make_async_remote_copy(
        src_ref=src, dst_ref=dst, send_sem=sends.at[at], recv_sem=recvs.at[at],
        device_id={axis: target}, device_id_type=MESH,
    )


def spread_kernel(peers, n, x_ref, h_ref, all_ref, fl_ref, fr_ref, sends, recvs, z_sends, z_recvs, own_sem):
    k, me = lax.axis_index("dp"), lax.axis_index("mp")
    bits = peers.bit_length() - 1
    barrier = pltpu.get_barrier_semaphore()

    def flip(i, b):
        return i + (1 << b) * (1 - 2 * ((i // (1 << b)) % 2))

    for b in range(bits):
        pl.semaphore_signal(barrier, inc=1, device_id={"dp": flip(k, b)}, device_id_type=MESH)
    for t in (1, n - 1):
        pl.semaphore_signal(barrier, inc=1, device_id={"mp": lax.rem(me + t, n)}, device_id_type=MESH)
    pl.semaphore_wait(barrier, bits + 2)

    to_right = remote(h_ref, fl_ref, z_sends, z_recvs, 0, "mp", lax.rem(me + 1, n))
    to_left = remote(h_ref, fr_ref, z_sends, z_recvs, 1, "mp", lax.rem(me + n - 1, n))

    @pl.when(me < n - 1)
    def _():
        to_right.start()

    @pl.when(me > 0)
    def _():
        to_left.start()

    own = pltpu.make_async_copy(x_ref, all_ref.at[k], own_sem)
    own.start()
    half = x_ref.shape[0] // 2
    orders = [list(range(bits - 1, -1, -1)), list(range(bits - 2, 0, -1)) + [bits - 1, 0]]
    plans = []
    for h, order in enumerate(orders):
        at, seen, stages = h * (peers - 1), [()], []
        for b in order:
            stage = []
            for flips in seen:
                stage.append((at, flips, b))
                at += 1
            stages.append(stage)
            seen = seen + [flips + (b,) for flips in seen]
        plans.append(stages)

    def copy(h, at, flips, b):
        rows = pl.ds(h * half, half)
        source = k
        for f in flips:
            source = flip(source, f)
        src = x_ref.at[rows] if not flips else all_ref.at[source, rows]
        return remote(src, all_ref.at[source, rows], sends, recvs, at, "dp", flip(k, b))

    def arrival(h, at, flips, b):
        rows = pl.ds(h * half, half)
        source = flip(k, b)
        for f in flips:
            source = flip(source, f)
        here = all_ref.at[source, rows]
        return remote(here, here, sends, recvs, at, "dp", flip(k, b))

    for i in range(bits):
        for h in range(2):
            for piece in plans[h][i]:
                copy(h, *piece).start()
        for h in range(2):
            for piece in plans[h][i]:
                arrival(h, *piece).wait_recv()
    for i in range(bits):
        for h in range(2):
            for piece in plans[h][i]:
                copy(h, *piece).wait_send()
    own.wait()

    @pl.when(me < n - 1)
    def _():
        to_right.wait_send()
        to_left.wait_recv()

    @pl.when(me > 0)
    def _():
        to_left.wait_send()
        to_right.wait_recv()


def spread(packed, hidden, peers, n):
    hbm = pl.BlockSpec(memory_space=pl.ANY)
    count = 2 * (peers - 1)
    dma = pltpu.SemaphoreType.DMA
    return pl.pallas_call(
        functools.partial(spread_kernel, peers, n),
        out_shape=(
            jax.ShapeDtypeStruct((peers,) + packed.shape, packed.dtype),
            jax.ShapeDtypeStruct(hidden.shape, hidden.dtype),
            jax.ShapeDtypeStruct(hidden.shape, hidden.dtype),
        ),
        in_specs=[hbm] * 2,
        out_specs=(hbm,) * 3,
        scratch_shapes=[dma((count,)), dma((count,)), dma((2,)), dma((2,)), dma(())],
        compiler_params=pltpu.CompilerParams(collective_id=0, has_side_effects=True),
    )(packed, hidden)


def line_kernel(n, pieces, r_in, l_in, r_parts, l_parts, rights, lefts, r_out, l_out, sends, recvs):
    me = lax.axis_index("mp")
    barrier = pltpu.get_barrier_semaphore()
    for t in (1, n - 1):
        pl.semaphore_signal(barrier, inc=1, device_id={"mp": lax.rem(me + t, n)}, device_id_type=MESH)
    pl.semaphore_wait(barrier, 2)

    @pl.when(me == 0)
    def _():
        rights[...] = jnp.zeros_like(rights)

    @pl.when(me == n - 1)
    def _():
        lefts[...] = jnp.zeros_like(lefts)

    sides = (
        (r_in, r_parts, rights, r_out, me, me + 1),
        (l_in, l_parts, lefts, l_out, n - 1 - me, me + n - 1),
    )

    def piece(d, s, q):
        _, _, landing, held, _, to = sides[d]
        low, size = pieces[q]
        rows = pl.ds(low, size)
        at = (d * (n - 2) + s) * len(pieces) + q
        return remote(held.at[s, rows], landing.at[s, rows], sends, recvs, at, "mp", lax.rem(to, n))

    for s in range(n - 2):
        for q, (low, size) in enumerate(pieces):
            rows = pl.ds(low, size)
            for d, (came, parts, landing, held, seat, _) in enumerate(sides):
                if s:
                    @pl.when(seat > 0)
                    def _():
                        piece(d, s - 1, q).wait_recv()

                @pl.when(seat < n - 1)
                def _():
                    adds = (s >= seat).astype(jnp.float32) if s else (seat == 0).astype(jnp.float32)
                    before = landing[s - 1, rows] if s else came[rows]
                    total = before.astype(jnp.float32) + parts[s, rows] * adds
                    held[s, rows] = total.astype(held.dtype)
                    piece(d, s, q).start()
    for s in range(n - 2):
        for q in range(len(pieces)):
            for d in range(2):
                seat = sides[d][4]
                if s == n - 3:
                    @pl.when(seat > 0)
                    def _():
                        piece(d, s, q).wait_recv()

                @pl.when(seat < n - 1)
                def _():
                    piece(d, s, q).wait_send()


def line(number, n, r_in, l_in, r_parts, l_parts):
    cap, cols = r_in.shape
    units, many = cap // 16, 3
    cuts = [16 * (units * q // many) for q in range(many + 1)]
    pieces = [(a, b - a) for a, b in zip(cuts[:-1], cuts[1:])]
    vmem = pl.BlockSpec(memory_space=pltpu.VMEM)
    count = 2 * (n - 2) * many
    blocks = (n - 2, cap, cols)
    shape = jax.ShapeDtypeStruct(blocks, r_in.dtype)
    return pl.pallas_call(
        functools.partial(line_kernel, n, pieces),
        out_shape=(shape, shape),
        in_specs=[vmem] * 4,
        out_specs=(vmem, vmem),
        scratch_shapes=[
            pltpu.VMEM(blocks, r_in.dtype), pltpu.VMEM(blocks, r_in.dtype),
            pltpu.SemaphoreType.DMA((count,)), pltpu.SemaphoreType.DMA((count,)),
        ],
        compiler_params=pltpu.CompilerParams(
            collective_id=number, has_side_effects=True, vmem_limit_bytes=44 << 20
        ),
    )(r_in, l_in, r_parts, l_parts)


def shards(sample_grad, advantage, route_rows, route_count, gate_pre, up_pre, down_weight):
    learners, n = lax.axis_size("dp"), lax.axis_size("mp")
    me = lax.axis_index("mp")
    width = SLOTS // learners
    per = learners // n
    rows = gate_pre.shape[0]
    right = [(i, i + 1) for i in range(n - 1)]
    left = [(i + 1, i) for i in range(n - 1)]

    gate_in = gate_pre.astype(jnp.float32)
    up_in = up_pre.astype(jnp.float32)
    hidden = (gate_in * jax.nn.sigmoid(gate_in) * up_in).astype(jnp.bfloat16)

    weights = advantage.astype(jnp.float32) * (1.0 / 4096.0)
    scaled = (sample_grad.astype(jnp.float32) * weights[:, None]).astype(jnp.bfloat16)
    own_count = route_count[0]
    own_start = ends_of(own_count) - own_count
    spot = iota((learners, width), 1)
    place = jnp.where(spot < own_count[:, None], own_start[:, None] + spot, -1).reshape(-1)
    table = route_rows[0, :SLOTS]
    source = jnp.sum(jnp.where(iota((LIVE, SLOTS), 0) == place[None, :], table[None, :], 0), axis=1)
    packed = pick(source[:, None] == iota((LIVE, scaled.shape[0]), 1), scaled)
    tail = jnp.pad(own_count.astype(jnp.bfloat16)[None, :], ((0, SENT - LIVE - 1), (0, scaled.shape[1] - learners)))
    everything, from_left, from_right = spread(jnp.concatenate([packed, tail]), hidden, learners, n)

    counts = everything[:, LIVE, :learners].astype(jnp.int32)
    everything = everything.reshape(learners * SENT, -1)
    ends = ends_of(counts)

    p = iota((learners, learners, SENT), 2)
    begin = (ends - counts).T[:, :, None]
    finish = ends.T[:, :, None]
    inside = (p >= begin) & (p < finish)
    to_block = jnp.sum(jnp.where(inside, iota(p.shape, 0) // per + 1, 0), axis=0).reshape(-1) - 1
    to_rank = jnp.sum(jnp.where(inside, iota(p.shape, 0) % per * SLOTS + iota(p.shape, 1) * width + p - begin, 0), axis=0).reshape(-1)

    order = [1, n - 1] + [t for t in range(2, n - 1)] + [0]
    first = 2

    def body(number, cap):
        def run(hidden, from_left, from_right, everything, to_block, to_rank, gate_pre, up_pre, down_weight):
            kept = {0: hidden}
            r_in, l_in = from_left, from_right

            def slots_of(positions):
                held = [
                    (to_block == (me - t) % n)[None, :] & (iota((cap, to_rank.shape[0]), 0) == to_rank[None, :])
                    for t in positions
                ]
                return pick(jnp.concatenate(held), everything)

            slots_a = slots_of(order[:first])
            part_a = lax.optimization_barrier(dot(slots_a, down_weight, 1, 1))
            slots_b = slots_of(order[first:])
            part_b = lax.optimization_barrier(dot(slots_b, down_weight, 1, 1))
            partial = {}
            for i, t in enumerate(order):
                held = part_a if i < first else part_b
                at = (i if i < first else i - first) * cap
                partial[t] = held[at:at + cap]

            def load(came, position, adds):
                own = jnp.where(adds, partial[position], 0.0)
                return (came.astype(jnp.float32) + own).astype(jnp.bfloat16)

            rights, lefts = {1: r_in}, {1: l_in}
            if LINE:
                r_parts = jnp.stack([partial[t] for t in range(1, n - 1)])
                l_parts = jnp.stack([partial[n - t] for t in range(1, n - 1)])
                r_all, l_all = line(number + 1, n, jnp.where(me > 0, r_in, 0), jnp.where(me < n - 1, l_in, 0), r_parts, l_parts)
                for step in range(2, n):
                    rights[step], lefts[step] = r_all[step - 2], l_all[step - 2]
            for step in range(n if LINE else 2, n + 1):
                r_out = load(jnp.where(me > 0, rights[step - 1], 0), step - 1, step >= me + 2)
                l_out = load(jnp.where(me < n - 1, lefts[step - 1], 0), n + 1 - step, step >= n - me + 1)
                rights[step] = lax.ppermute(r_out, "mp", right)
                lefts[step] = lax.ppermute(l_out, "mp", left)
            for t in range(1, n):
                kept[t] = jnp.where(me >= t, rights[t], lefts[n - t])
            hidden_all = jnp.concatenate([kept[t] for t in order])
            grad_down = dot(hidden_all, jnp.concatenate([slots_a, slots_b]), 0, 0)

            hidden_grad = partial[0] + rights[n].astype(jnp.float32) + lefts[n].astype(jnp.float32)
            gate_in = gate_pre.astype(jnp.float32)
            up_in = up_pre.astype(jnp.float32)
            s = jax.nn.sigmoid(gate_in)
            grad_gate = (hidden_grad * up_in * (s * (1.0 + gate_in * (1.0 - s)))).astype(jnp.bfloat16)
            grad_up = (hidden_grad * (gate_in * s)).astype(jnp.bfloat16)
            return grad_down, grad_gate, grad_up

        return run

    return body(0, rows)(
        hidden, from_left, from_right, everything, to_block, to_rank, gate_pre, up_pre, down_weight
    )


def solution(mesh):
    placed = (
        P("dp", "mp"),
        P("dp"),
        P("dp", None),
        P("dp", None),
        P("mp", "dp"),
        P("mp", "dp"),
        P("dp", "mp"),
    )
    return jax.shard_map(
        shards,
        mesh=mesh,
        in_specs=placed,
        out_specs=(P("dp", "mp"), P("mp", "dp"), P("mp", "dp")),
        check_vma=False,
    )
```
